32 devices in a mesh: groups: 2 (over y), wide: 4 (over z), narrow: 2 (over x), pol: 2 (over core).
Axes of the slice: x: 2, y: 2, z: 4, core: 2. Of those that a mesh axis runs over, the one named last changes fastest.
Arguments:
- voltages: bfloat16 [1024, 12288], P(('groups', 'narrow', 'pol'), 'wide'), parts along dimension 0, may hold values from -6 to 6
- pfb_window: float32 [4, 1024], replicated, may hold values from -0.25 to 0.25
- tile_pairs: int32 [3, 2], replicated, may hold values from 0 to 1, as said below
- assign: int32 [4, 1], replicated, may hold values from -1 to 2, as said below
Outputs:
- visibility: bfloat16 [8, 16, 256, 2, 256], P(('groups', 'wide'), ('narrow', 'pol')), parts along dimension 0
The draws below stay inside these ranges and needn't reach their ends.
There are 2 independent parts, one for each index of `groups`. The reference program is written for one: setup_inputs(seed, part) draws one part's arguments, and reference() takes and returns one part's arrays. A program takes and returns all parts, laid end to end along the dimension named above; an argument that names none is the same for every part. Nothing has to cross between parts.
Inputs may be any that keep to these rules, and one draw needn't show every extreme that they name: `tile_pairs`: each row lists a distinct pair of blocks with row <= column; every such pair of the 2 blocks appears in exactly one row. `assign`: every tile number 0 .. 2 appears exactly once in the table; in each row the tile numbers come first and the remaining entries are -1; some row holds 1 tiles.
All inputs are finite; a program needn't handle non-finite values.
Results may differ from the reference program's by a relative error of at most 0.0062.
Values may be sent and summed in bfloat16 or wider, within the bound.
A program may use at most 128 MiB of HBM per device.

```python
import math
import jax
import jax.numpy as jnp
import numpy as np
from jax import lax

CHAN = 512
NFFT = 1024
OUTCH = 16
AVG = 32
TAPS = 4
BLOCK = 256
SPECTRA = 12
SAMPLES = 12288
INPUTS = 512
NBLK = 2
NTILES = 3
MOST = 1
N_WIDE = 4


def draw_tile_pairs(key, part):
    key = jax.random.fold_in(key, 11)
    upper_pairs = np.array([(first_block, second_block) for first_block in range(NBLK) for second_block in range(first_block, NBLK)], dtype=np.int32)
    ordering = jax.random.permutation(key, NTILES)
    return jnp.asarray(upper_pairs)[ordering]


def draw_assign(key, part):
    key = jax.random.fold_in(key, 23)
    slots_total = N_WIDE * MOST
    score_key, heavy_key, order_key = jax.random.split(key, 3)
    scores = jax.random.randint(score_key, (slots_total,), 0, 1 << 20) * slots_total + jnp.arange(slots_total, dtype=jnp.int32)
    heavy = jax.random.randint(heavy_key, (), 0, N_WIDE)
    owner_of = jnp.arange(slots_total, dtype=jnp.int32) // MOST
    scores = scores + jnp.where(owner_of == heavy, 1 << 28, 0).astype(jnp.int32)
    top_scores, chosen = lax.top_k(scores, NTILES)
    picked = jnp.zeros((slots_total,), jnp.int32).at[chosen].set(1)
    within = (jnp.cumsum(picked.reshape(N_WIDE, MOST), axis=1) - 1).reshape(-1)
    overall = jnp.cumsum(picked) - 1
    ordering = jax.random.permutation(order_key, NTILES)
    numbers = ordering[jnp.clip(overall, 0, NTILES - 1)]
    target = jnp.where(picked == 1, owner_of * MOST + within, slots_total)
    table = jnp.full((slots_total,), -1, jnp.int32).at[target].set(numbers.astype(jnp.int32), mode='drop')
    return table.reshape(N_WIDE, MOST)


def levels(stream_key, shape, cuts, low, largest):
    def one(position, parts):
        heights = jax.random.uniform(jax.random.fold_in(jax.random.fold_in(stream_key, 6), position), (parts,), jnp.float32, low / len(cuts), largest / len(cuts))
        return jnp.repeat(jnp.exp(heights), shape[position] // parts).reshape((-1,) + (1,) * (len(shape) - position - 1))

    level = one(*cuts[0])
    for cut in cuts[1:]:
        level = level * one(*cut)
    return level


def noise(rng, shape, spread, bound, cuts=(), held_as=jnp.bfloat16):
    values = spread * jax.random.normal(rng, shape, jnp.float32)
    if cuts:
        values = values * levels(rng, shape, cuts, -0.22, 0.18)
    return jnp.clip(values, -bound, bound).astype(held_as)


def setup_inputs(seed: int = 0, part: int = 0) -> dict:
    key_of = jax.random.split(jax.random.key(seed), 5)
    own_keys = jax.random.split(jax.random.fold_in(key_of[4], part), 5)
    return {
        "voltages": noise(own_keys[0], (INPUTS, SAMPLES), 1.0, 6.0, ((0, 4), (1, 4))),
        "pfb_window": noise(key_of[1], (TAPS, NFFT), ((TAPS * NFFT) ** -0.5), 0.25, (), jnp.float32),
        "tile_pairs": draw_tile_pairs(jax.random.fold_in(key_of[4], 71), part),
        "assign": draw_assign(jax.random.fold_in(key_of[4], 71), part),
    }


def fourier_table(length, channels):
    sample_pos = jnp.arange(length, dtype=jnp.int32)[:, None]
    channel_pos = jnp.arange(channels, dtype=jnp.int32)[None, :]
    phase = ((sample_pos * channel_pos) % length).astype(jnp.float32) * (2.0 * math.pi / length)
    table = jnp.stack([jnp.cos(phase), -jnp.sin(phase)], axis=2)
    return table.reshape(length, 2 * channels).astype(jnp.bfloat16)


def reference(voltages, pfb_window, tile_pairs, assign):
    frames = voltages.astype(jnp.float32).reshape(INPUTS, SPECTRA, NFFT)
    padded = jnp.concatenate([jnp.zeros((INPUTS, TAPS - 1, NFFT), jnp.float32), frames], axis=1)
    filtered = pfb_window[0] * padded[:, 0:SPECTRA]
    for tap_index in range(1, TAPS):
        filtered = filtered + pfb_window[tap_index] * padded[:, tap_index:tap_index + SPECTRA]
    filtered = filtered.astype(jnp.bfloat16)
    table = fourier_table(NFFT, CHAN)
    spectra = jnp.dot(filtered.reshape(INPUTS * SPECTRA, NFFT), table, preferred_element_type=jnp.float32)
    spectra = spectra.astype(jnp.bfloat16)
    arranged = spectra.reshape(INPUTS, SPECTRA, CHAN, 2).transpose(2, 3, 1, 0)

    def one_tile(pair):
        left = lax.dynamic_slice_in_dim(arranged, (pair[0] * BLOCK).astype(jnp.int32), BLOCK, 3).astype(jnp.float32)
        right = lax.dynamic_slice_in_dim(arranged, (pair[1] * BLOCK).astype(jnp.int32), BLOCK, 3).astype(jnp.float32)
        turned = jnp.stack([-right[:, 1], right[:, 0]], axis=1)
        combined = jnp.concatenate([right, turned], axis=3)
        left_g = left.reshape(OUTCH, AVG, 2, SPECTRA, BLOCK)
        combined_g = combined.reshape(OUTCH, AVG, 2, SPECTRA, 2 * BLOCK)
        product = jnp.einsum("ocrsi,ocrsj->oij", left_g, combined_g, precision=lax.Precision.HIGHEST)
        return (product * (1.0 / (SPECTRA * AVG))).reshape(OUTCH, BLOCK, 2, BLOCK).astype(jnp.bfloat16)

    tiles = lax.map(one_tile, tile_pairs)
    flat_slots = assign.reshape(-1)
    chosen = tiles[jnp.maximum(flat_slots, 0)]
    live = (flat_slots >= 0)[:, None, None, None, None]
    return jnp.where(live, chosen, jnp.zeros_like(chosen))
```

```python
import functools
import math

import jax
import jax.numpy as jnp
import ml_dtypes
import numpy as np
from jax import lax
from jax.experimental import pallas as pl
from jax.experimental.pallas import tpu as pltpu
from jax.sharding import PartitionSpec as P

CHAN = 512
OUTCH = 16
BLOCK = 256
MESH = pl.DeviceIdType.MESH
CHUNKS = 4


def passed_along(block, axis, distance):
    devices = range(lax.axis_size(axis))
    route = [(i - distance, i) for i in devices if i - distance in devices]
    return lax.ppermute(block, axis, route)


def fourier_table(length, channels):
    sample_pos = jnp.arange(length, dtype=jnp.int32)[:, None]
    channel_pos = jnp.arange(channels, dtype=jnp.int32)[None, :]
    phase = (sample_pos * channel_pos % length).astype(jnp.float32) * (2.0 * math.pi / length)
    table = jnp.stack([jnp.cos(phase), -jnp.sin(phase)], axis=2)
    return table.reshape(length, 2 * channels).astype(jnp.bfloat16)


def tile_product(samples_in, tile_pairs, tile_number, block_width, averaged):
    safe_number = jnp.maximum(tile_number, 0)
    block_row = tile_pairs[safe_number, 0]
    block_column = tile_pairs[safe_number, 1]
    left = lax.dynamic_slice_in_dim(samples_in, block_row * block_width, block_width, 3)
    right = lax.dynamic_slice_in_dim(samples_in, block_column * block_width, block_width, 3)
    turned = jnp.stack([-right[:, 1], right[:, 0]], axis=1)
    combined = jnp.concatenate([right, turned], axis=3)
    outputs_here = left.shape[0] // averaged
    left_g = left.reshape(outputs_here, averaged, 2, left.shape[2], block_width)
    combined_g = combined.reshape(outputs_here, averaged, 2, left.shape[2], 2 * block_width)
    return jnp.einsum("ocrsi,ocrsj->oij", left_g, combined_g, preferred_element_type=jnp.float32)


def on_device(voltages, pfb_window, tile_pairs, assign):
    taps, length = pfb_window.shape
    channels = length // 2
    block_width = BLOCK
    averaged = CHAN // OUTCH
    history_rim = passed_along(voltages, "wide", 1)
    extended = jnp.concatenate([history_rim, voltages], axis=1).astype(jnp.float32)
    frames = extended.reshape(voltages.shape[0], -1, length)
    spectra_here = frames.shape[1] - taps + 1
    filtered = pfb_window[0] * frames[:, 0:spectra_here]
    for tap_index in range(1, taps):
        filtered = (
            filtered + pfb_window[tap_index] * frames[:, tap_index : tap_index + spectra_here]
        )
    filtered = filtered.astype(jnp.bfloat16)
    table = fourier_table(length, channels)
    spectra = jnp.einsum("imk,kq->qmi", filtered, table, preferred_element_type=jnp.float32).astype(
        jnp.bfloat16
    )
    moved = lax.all_to_all(
        spectra[:, :, None, :], ("narrow", "pol"), split_axis=0, concat_axis=2, tiled=True
    )
    arranged = moved.reshape(moved.shape[0] // 2, 2, spectra_here, -1)
    outputs_here = arranged.shape[0] // averaged
    position = lax.axis_index("wide")
    wide_count = lax.axis_size("wide")
    slots = assign.shape[1]
    own_row = lax.dynamic_index_in_dim(assign, position, 0, keepdims=False)
    scale = 1.0 / (wide_count * spectra_here * averaged)
    blank = jnp.zeros((outputs_here, block_width, 2 * block_width), jnp.float32)
    whole = lax.all_gather(arranged, "wide", axis=2, tiled=True)
    results = []
    for slot_index in range(slots):
        results.append(
            lax.cond(
                own_row[slot_index] >= 0,
                lambda number: tile_product(whole, tile_pairs, number, block_width, averaged),
                lambda number: blank,
                own_row[slot_index],
            )
        )
    totals = jnp.stack(results)
    visible = (
        (totals * scale)
        .reshape(slots, outputs_here, block_width, 2, block_width)
        .astype(jnp.bfloat16)
    )
    return visible


def table_constant(length, parts):
    channels = length // 2
    pos = np.arange(length, dtype=np.int64)[:, None] * np.arange(channels, dtype=np.int64)[None, :]
    phase = (pos % length).astype(np.float64) * (2.0 * math.pi / length)
    both = np.stack([np.cos(phase), -np.sin(phase)], axis=1)
    both = both.reshape(length, 2, parts, channels // parts).transpose(0, 2, 1, 3)
    return both.reshape(length, 2 * channels).astype(ml_dtypes.bfloat16)


def correlator(
    sizes,
    volt_ref, window_ref, table_hbm, pairs_ref, assign_ref,
    out_ref,
    raw, table, filt, stage, spec, total,
    load_sem, zsend, zrecv, xsend, xrecv,
):
    nz, nx, npol, rows, taps, length, averaged = sizes
    nd = nx * npol
    part = length // nd
    half = part // 2
    frames = volt_ref.shape[1] // length
    chunk = rows // CHUNKS
    z = lax.axis_index("wide")
    x = lax.axis_index("narrow")
    c = lax.axis_index("pol")
    me = x * npol + c

    load_v = pltpu.make_async_copy(volt_ref, raw.at[z], load_sem.at[0])
    load_t = pltpu.make_async_copy(table_hbm, table, load_sem.at[1])
    load_v.start()
    load_t.start()

    def peer(j):
        other = lax.rem(me + j, nd)
        return other, {"narrow": lax.div(other, npol), "pol": lax.rem(other, npol)}

    barrier = pltpu.get_barrier_semaphore()
    for j in range(1, nd):
        pl.semaphore_signal(barrier, inc=1, device_id=peer(j)[1], device_id_type=MESH)

    @pl.when(z > 0)
    def _():
        pl.semaphore_signal(barrier, inc=1, device_id={"wide": z - 1}, device_id_type=MESH)

    @pl.when(z < nz - 1)
    def _():
        pl.semaphore_signal(barrier, inc=1, device_id={"wide": z + 1}, device_id_type=MESH)

    near = (z > 0).astype(jnp.int32) + (z < nz - 1).astype(jnp.int32)
    pl.semaphore_wait(barrier, nd - 1 + near)

    def along(direction, s, r):
        rs = pl.ds(pl.multiple_of(r * chunk, chunk), chunk)
        target = z + 1 if direction == 0 else z - 1
        return pltpu.make_async_remote_copy(
            src_ref=raw.at[s, rs, :],
            dst_ref=raw.at[s, rs, :],
            send_sem=zsend.at[direction, s, r],
            recv_sem=zrecv.at[s, r],
            device_id={"wide": target},
            device_id_type=MESH,
        )

    def across(j, s, r, src=None):
        rs = pl.ds(pl.multiple_of(r * chunk, chunk), chunk)
        other, device = peer(j)
        sender = me if src is None else src
        return pltpu.make_async_remote_copy(
            src_ref=stage.at[s, other, :, rs, :],
            dst_ref=spec.at[s, sender, :, rs, :],
            send_sem=xsend.at[s, r, j],
            recv_sem=xrecv.at[s, r, sender],
            device_id=device,
            device_id_type=MESH,
        )

    load_v.wait()

    def own(r, _):
        @pl.when(z < nz - 1)
        def _():
            along(0, z, r).start()

        @pl.when(z > 0)
        def _():
            along(1, z, r).start()

        return 0

    lax.fori_loop(0, CHUNKS, own, 0)
    total[...] = jnp.zeros_like(total)
    load_t.wait()

    def channelize(s, r):
        rs = pl.ds(pl.multiple_of(r * chunk, chunk), chunk)
        earlier = jnp.maximum(s - 1, 0)
        live = jnp.where(s > 0, 1.0, 0.0).astype(jnp.float32)
        wide = 256
        for k in range(0, length, wide):
            part_of = []
            for f in range(frames):
                part_of.append(raw[earlier, rs, f * length + k : f * length + k + wide].astype(jnp.float32) * live)
            for f in range(frames):
                part_of.append(raw[s, rs, f * length + k : f * length + k + wide].astype(jnp.float32))
            for m in range(frames):
                first = frames + m - (taps - 1)
                value = window_ref[0:1, k : k + wide] * part_of[first]
                for t in range(1, taps):
                    value = value + window_ref[t : t + 1, k : k + wide] * part_of[first + t]
                filt[m * chunk : (m + 1) * chunk, k : k + wide] = value.astype(jnp.bfloat16)
        for d in range(nd):
            out = jnp.dot(
                filt[...], table[:, d * part : (d + 1) * part], preferred_element_type=jnp.float32
            ).astype(jnp.bfloat16)
            stage[s, d, :, rs, :] = out.reshape(frames, chunk, part)
        for j in range(1, nd):
            across(j, s, r).start()
        spec[s, me, :, rs, :] = stage[s, me, :, rs, :]

    number = assign_ref[z, 0]
    safe = jnp.maximum(number, 0)
    row = pairs_ref[safe, 0]
    column = pairs_ref[safe, 1]
    per_block = BLOCK // rows

    def correlate(s):
        for j in range(1, nd):
            src = lax.rem(me + j, nd)
            for r in range(CHUNKS):
                across(j, s, r, src).wait_recv()
        lane = lax.broadcasted_iota(jnp.int32, (1, part), 1)
        lane = jnp.where(lane >= half, lane - half, lane)
        for m in range(frames):
            left = right = None
            for b in range(nd // per_block):
                block = spec[s, b * per_block : (b + 1) * per_block, m].reshape(BLOCK, part)
                left = block if b == 0 else jnp.where(row == b, block, left)
                right = block if b == 0 else jnp.where(column == b, block, right)
            turned = jnp.concatenate([-right[:, half:], right[:, :half]], axis=1)
            for o in range(half // averaged):
                keep = jnp.where((lane >= o * averaged) & (lane < (o + 1) * averaged), 1.0, 0.0)
                kept = left * keep.astype(jnp.bfloat16)
                for side, value in ((0, right), (1, turned)):
                    total[o, :, side * BLOCK : (side + 1) * BLOCK] += lax.dot_general(
                        kept, value, (((1,), (1,)), ((), ())), preferred_element_type=jnp.float32
                    )

    def candidate(d, i):
        s = jnp.where(i == 0, z - d + 1, jnp.where(i == 1, 0, z + d))
        valid = jnp.where(
            i == 0,
            jnp.logical_and(d > 0, z - d >= 0).astype(jnp.int32),
            jnp.where(i == 1, (z == d).astype(jnp.int32), jnp.logical_and(d > 0, z + d < nz).astype(jnp.int32)),
        )
        return jnp.clip(s, 0, nz - 1), valid

    def step(d, _):
        def arrive(r, _):
            @pl.when(jnp.logical_and(d > 0, z - d >= 0))
            def _():
                along(0, z - d, r).wait_recv()

                @pl.when(z < nz - 1)
                def _():
                    along(0, z - d, r).start()

            @pl.when(jnp.logical_and(d > 0, z + d < nz))
            def _():
                along(1, z + d, r).wait_recv()

                @pl.when(z > 0)
                def _():
                    along(1, z + d, r).start()

            def one(i, _):
                s, valid = candidate(d, i)

                @pl.when(valid == 1)
                def _():
                    channelize(s, r)

                return 0

            lax.fori_loop(0, 3, one, 0)
            return 0

        @pl.when(d < nz)
        def _():
            lax.fori_loop(0, CHUNKS, arrive, 0)

        def add(i, _):
            s, valid = candidate(d - 1, i)

            @pl.when(jnp.logical_and(d > 0, valid == 1))
            def _():
                correlate(s)

            return 0

        lax.fori_loop(0, 3, add, 0)
        return 0

    lax.fori_loop(0, nz + 1, step, 0)

    scale = jnp.where(number >= 0, 1.0, 0.0).astype(jnp.float32) * (1.0 / (nz * frames * averaged))
    out_ref[...] = (total[...] * scale).astype(jnp.bfloat16)

    def drain(r, _):
        for s in range(nz):
            @pl.when(jnp.logical_and(z < nz - 1, s <= z))
            def _():
                along(0, s, r).wait_send()

            @pl.when(jnp.logical_and(z > 0, s >= z))
            def _():
                along(1, s, r).wait_send()

            for j in range(1, nd):
                across(j, s, r).wait_send()
        return 0

    lax.fori_loop(0, CHUNKS, drain, 0)


def fused(voltages, pfb_window, tile_pairs, assign):
    rows, samples = voltages.shape
    taps, length = pfb_window.shape
    nz, nx, npol = (lax.axis_size(a) for a in ("wide", "narrow", "pol"))
    nd = nx * npol
    frames = samples // length
    averaged = CHAN // OUTCH
    part = length // nd
    outs = part // 2 // averaged
    chunk = rows // CHUNKS
    sizes = (nz, nx, npol, rows, taps, length, averaged)
    visible = pl.pallas_call(
        functools.partial(correlator, sizes),
        out_shape=jax.ShapeDtypeStruct((outs, BLOCK, 2 * BLOCK), jnp.bfloat16),
        in_specs=[
            pl.BlockSpec(memory_space=pl.ANY),
            pl.BlockSpec(memory_space=pltpu.VMEM),
            pl.BlockSpec(memory_space=pl.ANY),
            pl.BlockSpec(memory_space=pltpu.SMEM),
            pl.BlockSpec(memory_space=pltpu.SMEM),
        ],
        out_specs=pl.BlockSpec(memory_space=pltpu.VMEM),
        scratch_shapes=[
            pltpu.VMEM((nz, rows, samples), jnp.bfloat16),
            pltpu.VMEM((length, length), jnp.bfloat16),
            pltpu.VMEM((frames * chunk, length), jnp.bfloat16),
            pltpu.VMEM((nz, nd, frames, rows, part), jnp.bfloat16),
            pltpu.VMEM((nz, nd, frames, rows, part), jnp.bfloat16),
            pltpu.VMEM((outs, BLOCK, 2 * BLOCK), jnp.float32),
            pltpu.SemaphoreType.DMA((2,)),
            pltpu.SemaphoreType.DMA((2, nz, CHUNKS)),
            pltpu.SemaphoreType.DMA((nz, CHUNKS)),
            pltpu.SemaphoreType.DMA((nz, CHUNKS, nd)),
            pltpu.SemaphoreType.DMA((nz, CHUNKS, nd)),
        ],
        compiler_params=pltpu.CompilerParams(
            collective_id=0, has_side_effects=True, vmem_limit_bytes=40 * 1024 * 1024
        ),
        cost_estimate=pl.CostEstimate(flops=10**10, bytes_accessed=10**7, transcendentals=0),
    )(voltages, pfb_window, jnp.asarray(table_constant(length, nd)), tile_pairs, assign)
    return visible.reshape(1, outs, BLOCK, 2, BLOCK)


def solution(mesh):
    in_specs = (P(("groups", "narrow", "pol"), "wide"), P(), P(), P())
    out_specs = P(("groups", "wide"), ("narrow", "pol"), None, None, None)

    def run(voltages, pfb_window, tile_pairs, assign):
        rows, samples = voltages.shape
        taps, length = pfb_window.shape
        part = length // (lax.axis_size("narrow") * lax.axis_size("pol"))
        fits = (
            part % 256 == 0
            and assign.shape[1] == 1
            and BLOCK % rows == 0
            and rows % (16 * CHUNKS) == 0
            and samples // length >= taps - 1
        )
        return (fused if fits else on_device)(voltages, pfb_window, tile_pairs, assign)

    return jax.shard_map(run, mesh=mesh, in_specs=in_specs, out_specs=out_specs, check_vma=False)
```

```python
import functools
import math

import jax
import jax.numpy as jnp
import ml_dtypes
import numpy as np
from jax import lax
from jax.experimental import pallas as pl
from jax.experimental.pallas import tpu as pltpu
from jax.sharding import PartitionSpec as P

CHAN = 512
OUTCH = 16
BLOCK = 256
MESH = pl.DeviceIdType.MESH
CHUNKS = 4


def passed_along(block, axis, distance):
    devices = range(lax.axis_size(axis))
    route = [(i - distance, i) for i in devices if i - distance in devices]
    return lax.ppermute(block, axis, route)


def fourier_table(length, channels):
    sample_pos = jnp.arange(length, dtype=jnp.int32)[:, None]
    channel_pos = jnp.arange(channels, dtype=jnp.int32)[None, :]
    phase = (sample_pos * channel_pos % length).astype(jnp.float32) * (2.0 * math.pi / length)
    table = jnp.stack([jnp.cos(phase), -jnp.sin(phase)], axis=2)
    return table.reshape(length, 2 * channels).astype(jnp.bfloat16)


def tile_product(samples_in, tile_pairs, tile_number, block_width, averaged):
    safe_number = jnp.maximum(tile_number, 0)
    block_row = tile_pairs[safe_number, 0]
    block_column = tile_pairs[safe_number, 1]
    left = lax.dynamic_slice_in_dim(samples_in, block_row * block_width, block_width, 3)
    right = lax.dynamic_slice_in_dim(samples_in, block_column * block_width, block_width, 3)
    turned = jnp.stack([-right[:, 1], right[:, 0]], axis=1)
    combined = jnp.concatenate([right, turned], axis=3)
    outputs_here = left.shape[0] // averaged
    left_g = left.reshape(outputs_here, averaged, 2, left.shape[2], block_width)
    combined_g = combined.reshape(outputs_here, averaged, 2, left.shape[2], 2 * block_width)
    return jnp.einsum("ocrsi,ocrsj->oij", left_g, combined_g, preferred_element_type=jnp.float32)


def on_device(voltages, pfb_window, tile_pairs, assign):
    taps, length = pfb_window.shape
    channels = length // 2
    block_width = BLOCK
    averaged = CHAN // OUTCH
    history_rim = passed_along(voltages, "wide", 1)
    extended = jnp.concatenate([history_rim, voltages], axis=1).astype(jnp.float32)
    frames = extended.reshape(voltages.shape[0], -1, length)
    spectra_here = frames.shape[1] - taps + 1
    filtered = pfb_window[0] * frames[:, 0:spectra_here]
    for tap_index in range(1, taps):
        filtered = (
            filtered + pfb_window[tap_index] * frames[:, tap_index : tap_index + spectra_here]
        )
    filtered = filtered.astype(jnp.bfloat16)
    table = fourier_table(length, channels)
    spectra = jnp.einsum("imk,kq->qmi", filtered, table, preferred_element_type=jnp.float32).astype(
        jnp.bfloat16
    )
    moved = lax.all_to_all(
        spectra[:, :, None, :], ("narrow", "pol"), split_axis=0, concat_axis=2, tiled=True
    )
    arranged = moved.reshape(moved.shape[0] // 2, 2, spectra_here, -1)
    outputs_here = arranged.shape[0] // averaged
    position = lax.axis_index("wide")
    wide_count = lax.axis_size("wide")
    slots = assign.shape[1]
    own_row = lax.dynamic_index_in_dim(assign, position, 0, keepdims=False)
    scale = 1.0 / (wide_count * spectra_here * averaged)
    blank = jnp.zeros((outputs_here, block_width, 2 * block_width), jnp.float32)
    whole = lax.all_gather(arranged, "wide", axis=2, tiled=True)
    results = []
    for slot_index in range(slots):
        results.append(
            lax.cond(
                own_row[slot_index] >= 0,
                lambda number: tile_product(whole, tile_pairs, number, block_width, averaged),
                lambda number: blank,
                own_row[slot_index],
            )
        )
    totals = jnp.stack(results)
    visible = (
        (totals * scale)
        .reshape(slots, outputs_here, block_width, 2, block_width)
        .astype(jnp.bfloat16)
    )
    return visible


def table_constant(length, parts):
    channels = length // 2
    pos = np.arange(length, dtype=np.int64)[:, None] * np.arange(channels, dtype=np.int64)[None, :]
    phase = (pos % length).astype(np.float64) * (2.0 * math.pi / length)
    both = np.stack([np.cos(phase), -np.sin(phase)], axis=1)
    both = both.reshape(length, 2, parts, channels // parts).transpose(0, 2, 1, 3)
    return both.reshape(length, 2 * channels).astype(ml_dtypes.bfloat16)


def correlator(
    sizes,
    volt_ref, window_hbm, table_hbm, pairs_ref, assign_ref,
    out_ref,
    raw, window_ref, table, filt, stage, spec, total,
    load_sem, zsend, zrecv, xsend, xrecv,
):
    nz, nx, npol, rows, taps, length, averaged = sizes
    nd = nx * npol
    part = length // nd
    half = part // 2
    frames = volt_ref.shape[1] // length
    chunk = rows // CHUNKS
    z = lax.axis_index("wide")
    x = lax.axis_index("narrow")
    c = lax.axis_index("pol")
    me = x * npol + c

    load_v = pltpu.make_async_copy(volt_ref, raw.at[z], load_sem.at[0])
    load_t = pltpu.make_async_copy(table_hbm, table, load_sem.at[1])
    load_w = pltpu.make_async_copy(window_hbm, window_ref, load_sem.at[2])
    load_v.start()
    load_w.start()
    load_t.start()

    def peer(j):
        other = lax.rem(me + j, nd)
        return other, {"narrow": lax.div(other, npol), "pol": lax.rem(other, npol)}

    barrier = pltpu.get_barrier_semaphore()
    for j in range(1, nd):
        pl.semaphore_signal(barrier, inc=1, device_id=peer(j)[1], device_id_type=MESH)

    @pl.when(z > 0)
    def _():
        pl.semaphore_signal(barrier, inc=1, device_id={"wide": z - 1}, device_id_type=MESH)

    @pl.when(z < nz - 1)
    def _():
        pl.semaphore_signal(barrier, inc=1, device_id={"wide": z + 1}, device_id_type=MESH)

    near = (z > 0).astype(jnp.int32) + (z < nz - 1).astype(jnp.int32)
    pl.semaphore_wait(barrier, nd - 1 + near)

    def along(direction, s, r):
        rs = pl.ds(pl.multiple_of(r * chunk, chunk), chunk)
        target = z + 1 if direction == 0 else z - 1
        return pltpu.make_async_remote_copy(
            src_ref=raw.at[s, rs, :],
            dst_ref=raw.at[s, rs, :],
            send_sem=zsend.at[direction, s, r],
            recv_sem=zrecv.at[s, r],
            device_id={"wide": target},
            device_id_type=MESH,
        )

    def across(j, s, r, src=None):
        rs = pl.ds(pl.multiple_of(r * chunk, chunk), chunk)
        other, device = peer(j)
        sender = me if src is None else src
        return pltpu.make_async_remote_copy(
            src_ref=stage.at[s, other, :, rs, :],
            dst_ref=spec.at[s, sender, :, rs, :],
            send_sem=xsend.at[s, r, j],
            recv_sem=xrecv.at[s, r, sender],
            device_id=device,
            device_id_type=MESH,
        )

    load_v.wait()

    def own(r, _):
        @pl.when(z < nz - 1)
        def _():
            along(0, z, r).start()

        @pl.when(z > 0)
        def _():
            along(1, z, r).start()

        return 0

    lax.fori_loop(0, CHUNKS, own, 0)
    total[...] = jnp.zeros_like(total)
    load_w.wait()
    load_t.wait()

    def channelize(s, r):
        rs = pl.ds(pl.multiple_of(r * chunk, chunk), chunk)
        earlier = jnp.maximum(s - 1, 0)
        live = jnp.where(s > 0, 1.0, 0.0).astype(jnp.float32)
        wide = 256
        for k in range(0, length, wide):
            part_of = []
            for f in range(frames):
                part_of.append(raw[earlier, rs, f * length + k : f * length + k + wide].astype(jnp.float32) * live)
            for f in range(frames):
                part_of.append(raw[s, rs, f * length + k : f * length + k + wide].astype(jnp.float32))
            for m in range(frames):
                first = frames + m - (taps - 1)
                value = window_ref[0:1, k : k + wide] * part_of[first]
                for t in range(1, taps):
                    value = value + window_ref[t : t + 1, k : k + wide] * part_of[first + t]
                filt[m * chunk : (m + 1) * chunk, k : k + wide] = value.astype(jnp.bfloat16)
        for d in range(nd):
            out = jnp.dot(
                filt[...], table[:, d * part : (d + 1) * part], preferred_element_type=jnp.float32
            ).astype(jnp.bfloat16)
            stage[s, d, :, rs, :] = out.reshape(frames, chunk, part)
        for j in range(1, nd):
            across(j, s, r).start()
        spec[s, me, :, rs, :] = stage[s, me, :, rs, :]

    number = assign_ref[0, z]
    safe = jnp.maximum(number, 0)
    row = pairs_ref[0, safe]
    column = pairs_ref[1, safe]
    per_block = BLOCK // rows

    def correlate(s):
        for j in range(1, nd):
            src = lax.rem(me + j, nd)
            for r in range(CHUNKS):
                across(j, s, r, src).wait_recv()
        lefts, rights, turned = [], [], []
        for m in range(frames):
            left = right = None
            for b in range(nd // per_block):
                block = spec[s, b * per_block : (b + 1) * per_block, m].reshape(BLOCK, part)
                left = block if b == 0 else jnp.where(row == b, block, left)
                right = block if b == 0 else jnp.where(column == b, block, right)
            lefts.append(left)
            rights.append(right)
            turned += [-right[:, half:], right[:, :half]]
        left = jnp.concatenate(lefts, axis=1)
        both = jnp.concatenate(
            [jnp.concatenate(rights, axis=1), jnp.concatenate(turned, axis=1)], axis=0
        )
        lane = lax.rem(lax.broadcasted_iota(jnp.int32, (1, frames * part), 1), half)
        for o in range(half // averaged):
            keep = jnp.where((lane >= o * averaged) & (lane < (o + 1) * averaged), 1.0, 0.0)
            total[o] += lax.dot_general(
                left * keep.astype(jnp.bfloat16),
                both,
                (((1,), (1,)), ((), ())),
                preferred_element_type=jnp.float32,
            )

    def candidate(d, i):
        s = jnp.where(i == 0, z - d + 1, jnp.where(i == 1, 0, z + d))
        valid = jnp.where(
            i == 0,
            jnp.logical_and(d > 0, z - d >= 0).astype(jnp.int32),
            jnp.where(i == 1, (z == d).astype(jnp.int32), jnp.logical_and(d > 0, z + d < nz).astype(jnp.int32)),
        )
        return jnp.clip(s, 0, nz - 1), valid

    def step(d, _):
        def arrive(r, _):
            @pl.when(jnp.logical_and(d > 0, z - d >= 0))
            def _():
                along(0, z - d, r).wait_recv()

                @pl.when(z < nz - 1)
                def _():
                    along(0, z - d, r).start()

            @pl.when(jnp.logical_and(d > 0, z + d < nz))
            def _():
                along(1, z + d, r).wait_recv()

                @pl.when(z > 0)
                def _():
                    along(1, z + d, r).start()

            def one(i, _):
                s, valid = candidate(d, i)

                @pl.when(valid == 1)
                def _():
                    channelize(s, r)

                return 0

            lax.fori_loop(0, 3, one, 0)

            def add(i, _):
                s, valid = candidate(d - 1, i)

                @pl.when(jnp.logical_and(d > 0, valid == 1))
                def _():
                    correlate(s)

                return 0

            @pl.when(r == 1)
            def _():
                lax.fori_loop(0, 3, add, 0)

            return 0

        lax.fori_loop(0, CHUNKS, arrive, 0)
        return 0

    lax.fori_loop(0, nz + 1, step, 0)

    scale = jnp.where(number >= 0, 1.0, 0.0).astype(jnp.float32) * (1.0 / (nz * frames * averaged))
    out_ref[...] = (total[...] * scale).astype(jnp.bfloat16)

    def drain(r, _):
        for s in range(nz):
            @pl.when(jnp.logical_and(z < nz - 1, s <= z))
            def _():
                along(0, s, r).wait_send()

            @pl.when(jnp.logical_and(z > 0, s >= z))
            def _():
                along(1, s, r).wait_send()

            for j in range(1, nd):
                across(j, s, r).wait_send()
        return 0

    lax.fori_loop(0, CHUNKS, drain, 0)


def fused(voltages, pfb_window, tile_pairs, assign):
    rows, samples = voltages.shape
    taps, length = pfb_window.shape
    nz, nx, npol = (lax.axis_size(a) for a in ("wide", "narrow", "pol"))
    nd = nx * npol
    frames = samples // length
    averaged = CHAN // OUTCH
    part = length // nd
    outs = part // 2 // averaged
    chunk = rows // CHUNKS
    sizes = (nz, nx, npol, rows, taps, length, averaged)
    visible = pl.pallas_call(
        functools.partial(correlator, sizes),
        out_shape=jax.ShapeDtypeStruct((outs, BLOCK, 2 * BLOCK), jnp.bfloat16),
        in_specs=[
            pl.BlockSpec(memory_space=pltpu.HBM),
            pl.BlockSpec(memory_space=pltpu.HBM),
            pl.BlockSpec(memory_space=pltpu.HBM),
            pl.BlockSpec(memory_space=pltpu.SMEM),
            pl.BlockSpec(memory_space=pltpu.SMEM),
        ],
        out_specs=pl.BlockSpec(memory_space=pltpu.VMEM),
        scratch_shapes=[
            pltpu.VMEM((nz, rows, samples), jnp.bfloat16),
            pltpu.VMEM((taps, length), jnp.float32),
            pltpu.VMEM((length, length), jnp.bfloat16),
            pltpu.VMEM((frames * chunk, length), jnp.bfloat16),
            pltpu.VMEM((nz, nd, frames, rows, part), jnp.bfloat16),
            pltpu.VMEM((nz, nd, frames, rows, part), jnp.bfloat16),
            pltpu.VMEM((outs, BLOCK, 2 * BLOCK), jnp.float32),
            pltpu.SemaphoreType.DMA((3,)),
            pltpu.SemaphoreType.DMA((2, nz, CHUNKS)),
            pltpu.SemaphoreType.DMA((nz, CHUNKS)),
            pltpu.SemaphoreType.DMA((nz, CHUNKS, nd)),
            pltpu.SemaphoreType.DMA((nz, CHUNKS, nd)),
        ],
        compiler_params=pltpu.CompilerParams(
            collective_id=0, has_side_effects=True, vmem_limit_bytes=40 * 1024 * 1024
        ),
        cost_estimate=pl.CostEstimate(flops=10**10, bytes_accessed=10**7, transcendentals=0),
    )(voltages, pfb_window, jnp.asarray(table_constant(length, nd)), tile_pairs.T, assign.T)
    return visible.reshape(1, outs, BLOCK, 2, BLOCK)


def solution(mesh):
    in_specs = (P(("groups", "narrow", "pol"), "wide"), P(), P(), P())
    out_specs = P(("groups", "wide"), ("narrow", "pol"), None, None, None)

    def run(voltages, pfb_window, tile_pairs, assign):
        rows, samples = voltages.shape
        taps, length = pfb_window.shape
        part = length // (lax.axis_size("narrow") * lax.axis_size("pol"))
        fits = (
            part % 256 == 0
            and assign.shape[1] == 1
            and BLOCK % rows == 0
            and rows % (16 * CHUNKS) == 0
            and samples // length >= taps - 1
        )
        return (fused if fits else on_device)(voltages, pfb_window, tile_pairs, assign)

    return jax.shard_map(run, mesh=mesh, in_specs=in_specs, out_specs=out_specs, check_vma=False)
```

```python
import functools
import math

import jax
import jax.numpy as jnp
import ml_dtypes
import numpy as np
from jax import lax
from jax.experimental import pallas as pl
from jax.experimental.pallas import tpu as pltpu
from jax.sharding import PartitionSpec as P

CHAN = 512
OUTCH = 16
BLOCK = 256
MESH = pl.DeviceIdType.MESH
SHARES = (1, 1, 1, 1)
CHUNKS = len(SHARES)


def passed_along(block, axis, distance):
    devices = range(lax.axis_size(axis))
    route = [(i - distance, i) for i in devices if i - distance in devices]
    return lax.ppermute(block, axis, route)


def fourier_table(length, channels):
    sample_pos = jnp.arange(length, dtype=jnp.int32)[:, None]
    channel_pos = jnp.arange(channels, dtype=jnp.int32)[None, :]
    phase = (sample_pos * channel_pos % length).astype(jnp.float32) * (2.0 * math.pi / length)
    table = jnp.stack([jnp.cos(phase), -jnp.sin(phase)], axis=2)
    return table.reshape(length, 2 * channels).astype(jnp.bfloat16)


def tile_product(samples_in, tile_pairs, tile_number, block_width, averaged):
    safe_number = jnp.maximum(tile_number, 0)
    block_row = tile_pairs[safe_number, 0]
    block_column = tile_pairs[safe_number, 1]
    left = lax.dynamic_slice_in_dim(samples_in, block_row * block_width, block_width, 3)
    right = lax.dynamic_slice_in_dim(samples_in, block_column * block_width, block_width, 3)
    turned = jnp.stack([-right[:, 1], right[:, 0]], axis=1)
    combined = jnp.concatenate([right, turned], axis=3)
    outputs_here = left.shape[0] // averaged
    left_g = left.reshape(outputs_here, averaged, 2, left.shape[2], block_width)
    combined_g = combined.reshape(outputs_here, averaged, 2, left.shape[2], 2 * block_width)
    return jnp.einsum("ocrsi,ocrsj->oij", left_g, combined_g, preferred_element_type=jnp.float32)


def on_device(voltages, pfb_window, tile_pairs, assign):
    taps, length = pfb_window.shape
    channels = length // 2
    block_width = BLOCK
    averaged = CHAN // OUTCH
    history_rim = passed_along(voltages, "wide", 1)
    extended = jnp.concatenate([history_rim, voltages], axis=1).astype(jnp.float32)
    frames = extended.reshape(voltages.shape[0], -1, length)
    spectra_here = frames.shape[1] - taps + 1
    filtered = pfb_window[0] * frames[:, 0:spectra_here]
    for tap_index in range(1, taps):
        filtered = (
            filtered + pfb_window[tap_index] * frames[:, tap_index : tap_index + spectra_here]
        )
    filtered = filtered.astype(jnp.bfloat16)
    table = fourier_table(length, channels)
    spectra = jnp.einsum("imk,kq->qmi", filtered, table, preferred_element_type=jnp.float32).astype(
        jnp.bfloat16
    )
    moved = lax.all_to_all(
        spectra[:, :, None, :], ("narrow", "pol"), split_axis=0, concat_axis=2, tiled=True
    )
    arranged = moved.reshape(moved.shape[0] // 2, 2, spectra_here, -1)
    outputs_here = arranged.shape[0] // averaged
    position = lax.axis_index("wide")
    wide_count = lax.axis_size("wide")
    slots = assign.shape[1]
    own_row = lax.dynamic_index_in_dim(assign, position, 0, keepdims=False)
    scale = 1.0 / (wide_count * spectra_here * averaged)
    blank = jnp.zeros((outputs_here, block_width, 2 * block_width), jnp.float32)
    whole = lax.all_gather(arranged, "wide", axis=2, tiled=True)
    results = []
    for slot_index in range(slots):
        results.append(
            lax.cond(
                own_row[slot_index] >= 0,
                lambda number: tile_product(whole, tile_pairs, number, block_width, averaged),
                lambda number: blank,
                own_row[slot_index],
            )
        )
    totals = jnp.stack(results)
    visible = (
        (totals * scale)
        .reshape(slots, outputs_here, block_width, 2, block_width)
        .astype(jnp.bfloat16)
    )
    return visible


def table_constant(length, parts):
    channels = length // 2
    pos = np.arange(length, dtype=np.int64)[:, None] * np.arange(channels, dtype=np.int64)[None, :]
    phase = (pos % length).astype(np.float64) * (2.0 * math.pi / length)
    both = np.stack([np.cos(phase), -np.sin(phase)], axis=1)
    both = both.reshape(length, 2, parts, channels // parts).transpose(0, 2, 1, 3)
    return both.reshape(length, 2 * channels).astype(ml_dtypes.bfloat16)


def correlator(
    sizes,
    volt_ref, window_hbm, table_hbm, pairs_ref, assign_ref,
    out_ref,
    raw, window_ref, table, filt, stage, spec, total,
    load_sem, zsend, zrecv, xsend, xrecv,
):
    nz, nx, npol, rows, taps, length, averaged = sizes
    nd = nx * npol
    part = length // nd
    half = part // 2
    frames = volt_ref.shape[1] // length
    unit = rows // sum(SHARES)
    pieces = [pl.ds(unit * sum(SHARES[:r]), unit * SHARES[r]) for r in range(CHUNKS)]
    z = lax.axis_index("wide")
    x = lax.axis_index("narrow")
    c = lax.axis_index("pol")
    me = x * npol + c

    load_v = pltpu.make_async_copy(volt_ref, raw.at[z], load_sem.at[0])
    load_t = pltpu.make_async_copy(table_hbm, table, load_sem.at[1])
    load_w = pltpu.make_async_copy(window_hbm, window_ref, load_sem.at[2])
    load_v.start()
    load_w.start()
    load_t.start()

    def peer(j):
        other = lax.rem(me + j, nd)
        return other, {"narrow": lax.div(other, npol), "pol": lax.rem(other, npol)}

    barrier = pltpu.get_barrier_semaphore()
    for j in range(1, nd):
        pl.semaphore_signal(barrier, inc=1, device_id=peer(j)[1], device_id_type=MESH)

    @pl.when(z > 0)
    def _():
        pl.semaphore_signal(barrier, inc=1, device_id={"wide": z - 1}, device_id_type=MESH)

    @pl.when(z < nz - 1)
    def _():
        pl.semaphore_signal(barrier, inc=1, device_id={"wide": z + 1}, device_id_type=MESH)

    near = (z > 0).astype(jnp.int32) + (z < nz - 1).astype(jnp.int32)
    pl.semaphore_wait(barrier, nd - 1 + near)

    def along(direction, s, r, first=False):
        rs = pieces[r]
        target = z + 1 if direction == 0 else z - 1
        return pltpu.make_async_remote_copy(
            src_ref=(volt_ref.at[rs, :] if first else raw.at[s, rs, :]),
            dst_ref=raw.at[s, rs, :],
            send_sem=zsend.at[direction, s, r],
            recv_sem=zrecv.at[s, r],
            device_id={"wide": target},
            device_id_type=MESH,
        )

    def across(j, s, r, src=None):
        rs = pieces[r]
        other, device = peer(j)
        sender = me if src is None else src
        return pltpu.make_async_remote_copy(
            src_ref=stage.at[s, other, :, rs, :],
            dst_ref=spec.at[s, sender, :, rs, :],
            send_sem=xsend.at[s, r, j],
            recv_sem=xrecv.at[s, r, sender],
            device_id=device,
            device_id_type=MESH,
        )

    def own(r):
        @pl.when(z < nz - 1)
        def _():
            along(0, z, r, True).start()

        @pl.when(z > 0)
        def _():
            along(1, z, r, True).start()

    for r in range(CHUNKS):
        own(r)
    total[...] = jnp.zeros_like(total)
    load_v.wait()
    load_w.wait()
    load_t.wait()

    def channelize(s, r):
        rs = pieces[r]
        chunk = unit * SHARES[r]
        earlier = jnp.maximum(s - 1, 0)
        live = jnp.where(s > 0, 1.0, 0.0).astype(jnp.float32)
        wide = 256
        for k in range(0, length, wide):
            part_of = []
            for f in range(frames):
                part_of.append(raw[earlier, rs, f * length + k : f * length + k + wide].astype(jnp.float32) * live)
            for f in range(frames):
                part_of.append(raw[s, rs, f * length + k : f * length + k + wide].astype(jnp.float32))
            for m in range(frames):
                first = frames + m - (taps - 1)
                value = window_ref[0:1, k : k + wide] * part_of[first]
                for t in range(1, taps):
                    value = value + window_ref[t : t + 1, k : k + wide] * part_of[first + t]
                filt[m * chunk : (m + 1) * chunk, k : k + wide] = value.astype(jnp.bfloat16)
        for d in range(nd):
            out = jnp.dot(
                filt[0 : frames * chunk], table[:, d * part : (d + 1) * part], preferred_element_type=jnp.float32
            ).astype(jnp.bfloat16)
            stage[s, d, :, rs, :] = out.reshape(frames, chunk, part)
        for j in range(1, nd):
            across(j, s, r).start()
        spec[s, me, :, rs, :] = stage[s, me, :, rs, :]

    number = assign_ref[0, z]
    safe = jnp.maximum(number, 0)
    row = pairs_ref[0, safe]
    column = pairs_ref[1, safe]
    per_block = BLOCK // rows

    def correlate(s):
        for j in range(1, nd):
            src = lax.rem(me + j, nd)
            for r in range(CHUNKS):
                across(j, s, r, src).wait_recv()
        lefts, rights, turned = [], [], []
        for m in range(frames):
            left = right = None
            for b in range(nd // per_block):
                block = spec[s, b * per_block : (b + 1) * per_block, m].reshape(BLOCK, part)
                left = block if b == 0 else jnp.where(row == b, block, left)
                right = block if b == 0 else jnp.where(column == b, block, right)
            lefts.append(left)
            rights.append(right)
            turned += [-right[:, half:], right[:, :half]]
        left = jnp.concatenate(lefts, axis=1)
        both = jnp.concatenate(
            [jnp.concatenate(rights, axis=1), jnp.concatenate(turned, axis=1)], axis=0
        )
        lane = lax.rem(lax.broadcasted_iota(jnp.int32, (1, frames * part), 1), half)
        for o in range(half // averaged):
            keep = jnp.where((lane >= o * averaged) & (lane < (o + 1) * averaged), 1.0, 0.0)
            total[o] += lax.dot_general(
                left * keep.astype(jnp.bfloat16),
                both,
                (((1,), (1,)), ((), ())),
                preferred_element_type=jnp.float32,
            )

    def candidate(d, i):
        s = jnp.where(i == 0, z - d + 1, jnp.where(i == 1, 0, z + d))
        valid = jnp.where(
            i == 0,
            jnp.logical_and(d > 0, z - d >= 0).astype(jnp.int32),
            jnp.where(i == 1, (z == d).astype(jnp.int32), jnp.logical_and(d > 0, z + d < nz).astype(jnp.int32)),
        )
        return jnp.clip(s, 0, nz - 1), valid

    def step(d, _):
        def arrive(r):
            @pl.when(jnp.logical_and(d > 0, z - d >= 0))
            def _():
                along(0, z - d, r).wait_recv()

                @pl.when(z < nz - 1)
                def _():
                    along(0, z - d, r).start()

            @pl.when(jnp.logical_and(d > 0, z + d < nz))
            def _():
                along(1, z + d, r).wait_recv()

                @pl.when(z > 0)
                def _():
                    along(1, z + d, r).start()

            def one(i, _):
                s, valid = candidate(d, i)

                @pl.when(valid == 1)
                def _():
                    channelize(s, r)

                return 0

            lax.fori_loop(0, 3, one, 0)

            def add(i, _):
                s, valid = candidate(d - 1, i)

                @pl.when(jnp.logical_and(d > 0, valid == 1))
                def _():
                    correlate(s)

                return 0

            if r == 1:
                lax.fori_loop(0, 3, add, 0)

        for r in range(CHUNKS):
            arrive(r)
        return 0

    lax.fori_loop(0, nz + 1, step, 0)

    scale = jnp.where(number >= 0, 1.0, 0.0).astype(jnp.float32) * (1.0 / (nz * frames * averaged))
    out_ref[...] = (total[...] * scale).astype(jnp.bfloat16)

    def drain(r):
        for s in range(nz):
            @pl.when(jnp.logical_and(z < nz - 1, s <= z))
            def _():
                along(0, s, r).wait_send()

            @pl.when(jnp.logical_and(z > 0, s >= z))
            def _():
                along(1, s, r).wait_send()

            for j in range(1, nd):
                across(j, s, r).wait_send()

    for r in range(CHUNKS):
        drain(r)


def fused(voltages, pfb_window, tile_pairs, assign):
    rows, samples = voltages.shape
    taps, length = pfb_window.shape
    nz, nx, npol = (lax.axis_size(a) for a in ("wide", "narrow", "pol"))
    nd = nx * npol
    frames = samples // length
    averaged = CHAN // OUTCH
    part = length // nd
    outs = part // 2 // averaged
    chunk = rows // sum(SHARES) * max(SHARES)
    sizes = (nz, nx, npol, rows, taps, length, averaged)
    visible = pl.pallas_call(
        functools.partial(correlator, sizes),
        out_shape=jax.ShapeDtypeStruct((outs, BLOCK, 2 * BLOCK), jnp.bfloat16),
        in_specs=[
            pl.BlockSpec(memory_space=pltpu.HBM),
            pl.BlockSpec(memory_space=pltpu.HBM),
            pl.BlockSpec(memory_space=pltpu.HBM),
            pl.BlockSpec(memory_space=pltpu.SMEM),
            pl.BlockSpec(memory_space=pltpu.SMEM),
        ],
        out_specs=pl.BlockSpec(memory_space=pltpu.VMEM),
        scratch_shapes=[
            pltpu.VMEM((nz, rows, samples), jnp.bfloat16),
            pltpu.VMEM((taps, length), jnp.float32),
            pltpu.VMEM((length, length), jnp.bfloat16),
            pltpu.VMEM((frames * chunk, length), jnp.bfloat16),
            pltpu.VMEM((nz, nd, frames, rows, part), jnp.bfloat16),
            pltpu.VMEM((nz, nd, frames, rows, part), jnp.bfloat16),
            pltpu.VMEM((outs, BLOCK, 2 * BLOCK), jnp.float32),
            pltpu.SemaphoreType.DMA((3,)),
            pltpu.SemaphoreType.DMA((2, nz, CHUNKS)),
            pltpu.SemaphoreType.DMA((nz, CHUNKS)),
            pltpu.SemaphoreType.DMA((nz, CHUNKS, nd)),
            pltpu.SemaphoreType.DMA((nz, CHUNKS, nd)),
        ],
        compiler_params=pltpu.CompilerParams(
            collective_id=0, has_side_effects=True, vmem_limit_bytes=60 * 1024 * 1024
        ),
        cost_estimate=pl.CostEstimate(flops=10**10, bytes_accessed=10**7, transcendentals=0),
    )(voltages, pfb_window, jnp.asarray(table_constant(length, nd)), tile_pairs.T, assign.T)
    return visible.reshape(1, outs, BLOCK, 2, BLOCK)


def solution(mesh):
    in_specs = (P(("groups", "narrow", "pol"), "wide"), P(), P(), P())
    out_specs = P(("groups", "wide"), ("narrow", "pol"), None, None, None)

    def run(voltages, pfb_window, tile_pairs, assign):
        rows, samples = voltages.shape
        taps, length = pfb_window.shape
        part = length // (lax.axis_size("narrow") * lax.axis_size("pol"))
        fits = (
            part % 256 == 0
            and assign.shape[1] == 1
            and BLOCK % rows == 0
            and rows % (16 * sum(SHARES)) == 0
            and samples // length >= taps - 1
        )
        return (fused if fits else on_device)(voltages, pfb_window, tile_pairs, assign)

    return jax.shard_map(run, mesh=mesh, in_specs=in_specs, out_specs=out_specs, check_vma=False)
```
